32 devices in a mesh: ka: 8 (over z, x), ha: 4 (over y, core).
Axes of the slice: x: 2, y: 2, z: 4, core: 2. Of those that a mesh axis runs over, the one named last changes fastest.
Arguments:
- green_row: bfloat16 [64, 256, 64, 128], P('ha', None, 'ka'), may hold values from -6 to 6
- screened: bfloat16 [64, 256, 64, 128], P('ha', 'ka'), may hold values from -6 to 6
- propagator: float32 [256, 64, 128], P(None, 'ka'), may hold values from -1.5 to 1.5
Outputs:
- new_row: bfloat16 [64, 256, 64, 128], P('ha', None, 'ka')
The draws below stay inside these ranges and needn't reach their ends.
All inputs are finite; a program needn't handle non-finite values.
Results may differ from the reference program's by a relative error of at most 0.008.
Values may be sent and summed in bfloat16 or wider, within the bound.
A program may use at most 512 MiB of HBM per device.

```python
import math
import jax
import jax.numpy as jnp
from jax import lax

NO = 16
NKX = 64
NKY = 64
S = 64
P_SIZE = 256
W = 128


def block_scale(key, shape, shards, smallest, largest):
    level, own = 1.0, jax.random.fold_in(key, 6)
    for position, parts in shards:
        steps = jnp.exp(jax.random.uniform(jax.random.fold_in(own, position), (parts,), jnp.float32, smallest / len(shards), largest / len(shards)))
        level = level * jnp.repeat(steps, shape[position] // parts).reshape([-1 if axis == position else 1 for axis in range(len(shape))])
    return level


def normal_values(stream_key, extent, scale, bound, cuts=(), held_as=jnp.bfloat16):
    factor_of = block_scale(stream_key, extent, cuts, -0.22, 0.18) if cuts else 1.0
    entries = jax.random.normal(stream_key, extent, jnp.float32) * scale * factor_of
    return jnp.minimum(jnp.maximum(entries, -bound), bound).astype(held_as)


def setup_inputs(seed: int = 0) -> dict:
    key_list = jax.random.split(jax.random.key(seed), 4)
    green_row = normal_values(key_list[0], (S, P_SIZE, NKX, W), 1.0, 6.0, ((0, 4), (2, 8)))
    screened = normal_values(key_list[1], (S, P_SIZE, NKX, W), 1.0, 6.0, ((0, 4), (1, 8)))
    propagator = normal_values(key_list[2], (P_SIZE, NKX, W), NO ** -0.5, 1.5, ((1, 8),), jnp.float32)
    return {"green_row": green_row, "screened": screened, "propagator": propagator}


step_size = 0.004

def tables(count):
    index = jnp.arange(count, dtype=jnp.int32)
    product = index[:, None] * index[None, :] % count
    angle = product.astype(jnp.float32) * (2.0 * math.pi / count)
    scale = 1.0 / math.sqrt(count)
    return ((jnp.cos(angle) * scale).astype(jnp.bfloat16), (jnp.sin(angle) * scale).astype(jnp.bfloat16))

def row_matrix(cosine, sine, forward):
    signed = sine if forward else -sine
    upper = jnp.concatenate([cosine, signed], axis=1)
    lower = jnp.concatenate([-signed, cosine], axis=1)
    return jnp.concatenate([upper, lower], axis=0)

def swap_halves(field):
    width = field.shape[-1] // 2
    return jnp.concatenate([field[..., width:], field[..., :width]], axis=-1)

def along_rows(field, matrix):
    return jnp.einsum('pxw,wv->pxv', field.astype(jnp.float32), matrix.astype(jnp.float32))

def along_columns(field, cosine, sine, forward):
    field32 = field.astype(jnp.float32)
    first = jnp.einsum('pxw,xz->pzw', field32, cosine.astype(jnp.float32))
    second = jnp.einsum('pxw,xz->pzw', field32, sine.astype(jnp.float32))
    width = field.shape[-1] // 2
    if forward:
        return jnp.concatenate([first[..., :width] - second[..., width:], first[..., width:] + second[..., :width]], axis=-1)
    return jnp.concatenate([first[..., :width] + second[..., width:], first[..., width:] - second[..., :width]], axis=-1)

def screen_product(space, screen):
    width = space.shape[-1] // 2
    screen32 = screen.astype(jnp.float32)
    space_re, space_im = (space[..., :width], space[..., width:])
    screen_re, screen_im = (screen32[..., :width], screen32[..., width:])
    return jnp.concatenate([space_re * screen_re - space_im * screen_im, space_re * screen_im + space_im * screen_re], axis=-1).astype(jnp.bfloat16)

def reference(green_row, screened, propagator):
    cos_y, sin_y = tables(NKY)
    cos_x, sin_x = tables(NKX)
    forward_y = row_matrix(cos_y, sin_y, True)
    inverse_y = row_matrix(cos_y, sin_y, False)
    half_width = NKY

    def accumulate(carry, items):
        green, screen = items
        half = along_rows(green, forward_y).astype(jnp.bfloat16)
        space = along_columns(half, cos_x, sin_x, True)
        product = screen_product(space, screen)
        back = along_columns(product, cos_x, sin_x, False).astype(jnp.bfloat16)
        sigma = along_rows(back, inverse_y).astype(jnp.bfloat16)
        sigma32 = sigma.astype(jnp.float32).reshape(NO, NO, NKX, 2 * NKY)
        green32 = green.astype(jnp.float32).reshape(NO, NO, NKX, 2 * NKY)
        direct = jnp.einsum('acxw,bcxw->abxw', sigma32, green32)
        crossed = jnp.einsum('acxw,bcxw->abxw', sigma32, swap_halves(green32))
        part = jnp.concatenate([direct[..., :half_width] + direct[..., half_width:], crossed[..., half_width:] - crossed[..., :half_width]], axis=-1)
        return (carry - step_size * part, None)
    start = jnp.zeros((NO, NO, NKX, 2 * NKY), jnp.float32)
    memory, unused = lax.scan(accumulate, start, (green_row, screened))
    kernel = (propagator.reshape(NO, NO, NKX, 2 * NKY) - memory).astype(jnp.bfloat16).astype(jnp.float32)

    def advance(green):
        green32 = green.astype(jnp.float32).reshape(NO, NO, NKX, 2 * NKY)
        direct = jnp.einsum('abxw,bcxw->acxw', kernel, green32)
        crossed = jnp.einsum('abxw,bcxw->acxw', kernel, swap_halves(green32))
        result = jnp.concatenate([direct[..., :half_width] - direct[..., half_width:], crossed[..., :half_width] + crossed[..., half_width:]], axis=-1)
        return result.astype(jnp.bfloat16).reshape(P_SIZE, NKX, 2 * NKY)
    return lax.map(advance, green_row)
```

```python
import functools
import math

import jax
import jax.numpy as jnp
from jax import lax
from jax.experimental import pallas as pl
from jax.experimental.pallas import tpu as pltpu
from jax.sharding import PartitionSpec as P

NO = 16
NKX = 64
NKY = 64
VMEM_LIMIT = 58 * 1024 * 1024


step_size = 0.004


def tables(count):
    index = jnp.arange(count, dtype=jnp.int32)
    product = index[:, None] * index[None, :] % count
    angle = product.astype(jnp.float32) * (2.0 * math.pi / count)
    scale = 1.0 / math.sqrt(count)
    return (
        (jnp.cos(angle) * scale).astype(jnp.bfloat16),
        (jnp.sin(angle) * scale).astype(jnp.bfloat16),
    )


def row_matrix(cosine, sine, forward):
    signed = sine if forward else -sine
    upper = jnp.concatenate([cosine, signed], axis=1)
    lower = jnp.concatenate([-signed, cosine], axis=1)
    return jnp.concatenate([upper, lower], axis=0)


def swap_columns(matrix):
    half = matrix.shape[1] // 2
    return jnp.concatenate([matrix[:, half:], matrix[:, :half]], axis=1)


def params(**more):
    return pltpu.CompilerParams(vmem_limit_bytes=VMEM_LIMIT, **more)


def cost(flops, bytes_accessed):
    return pl.CostEstimate(flops=flops, bytes_accessed=bytes_accessed, transcendentals=0)


def screened_block(field, screen_ref, forward_ref, inverse_ref, u, first, group, parts):
    full_x, width = screen_ref.shape[2:]
    xl = full_x // parts
    middle = width // 2
    low = lax.broadcasted_iota(jnp.int32, (full_x, width), 1) < middle
    field = field.astype(jnp.float32).reshape(parts, group, xl, width)
    backs = []
    for pair in range(0, group, 2):
        columns = []
        for k in (pair, pair + 1):
            x = field[:, k].reshape(full_x, width)
            turned = pltpu.roll(x, middle, 1)
            turned = jnp.where(low, -turned, turned)
            columns.append(jnp.concatenate([x, turned], axis=0).astype(jnp.bfloat16))
        stacked = jnp.concatenate(columns, axis=1)
        space = jnp.dot(forward_ref[...], stacked, preferred_element_type=jnp.float32)
        columns = []
        for j in range(2):
            s = space[:, j * width : (j + 1) * width]
            w = screen_ref[u, first + pair + j].astype(jnp.float32)
            direct = s * w
            crossed = s * pltpu.roll(w, middle, 1)
            moved = pltpu.roll(jnp.where(low, crossed, -direct), middle, 1)
            prod = jnp.where(low, direct, crossed) + moved
            turned = pltpu.roll(prod, middle, 1)
            turned = jnp.where(low, -turned, turned)
            columns.append(jnp.concatenate([prod, turned], axis=0).astype(jnp.bfloat16))
        stacked = jnp.concatenate(columns, axis=1)
        back = jnp.dot(inverse_ref[...], stacked, preferred_element_type=jnp.float32)
        for j in range(2):
            backs.append(back[:, j * width : (j + 1) * width].reshape(parts, 1, xl, width))
    out = jnp.concatenate(backs, axis=1).reshape(parts, group * xl, width)
    return out.astype(jnp.bfloat16)


def time_kernel(parts, hist, green, screened, base, forward_y, inverse_y, spread, forward_x, inverse_x):
    steps, rows, width = green.shape
    pairs = screened.shape[1]
    piece = rows // parts
    xl = rows // (NO * NO)
    group = min(16, pairs)
    ta, tb = 4, 8
    quarter = NO // hist
    qrows = rows // hist
    mesh_id = pl.DeviceIdType.MESH

    def body(
        green_ref, screen_ref, base_ref, fy_ref, iy_ref, spread_ref, fx_ref, ix_ref, out_ref,
        send, there, here, sig, gre, total, sums, final, send_sem, recv_sem, hsend_sem, hrecv_sem,
    ):
        me = lax.axis_index("ka")
        mine = lax.axis_index("ha")
        barrier = pltpu.get_barrier_semaphore()
        for k in range(1, parts):
            pl.semaphore_signal(
                barrier, inc=1, device_id={"ka": lax.rem(me + k, parts)}, device_id_type=mesh_id
            )
        for k in range(1, hist):
            pl.semaphore_signal(
                barrier, inc=1, device_id={"ha": lax.rem(mine + k, hist)}, device_id_type=mesh_id
            )
        pl.semaphore_wait(barrier, parts + hist - 2)

        def spread_out(phase, source, target, u):
            target[u, me] = source[u, me]
            for k in range(1, parts):
                other = lax.rem(me + k, parts)
                pltpu.make_async_remote_copy(
                    src_ref=source.at[u, other],
                    dst_ref=target.at[u, me],
                    send_sem=send_sem.at[phase, u],
                    recv_sem=recv_sem.at[phase, u],
                    device_id={"ka": other},
                    device_id_type=mesh_id,
                ).start()

        def wait_for(ref, count, sem):
            pltpu.make_async_copy(ref.at[pl.ds(0, count)], ref.at[pl.ds(0, count)], sem).wait()

        def forward(u, carry):
            half = jnp.dot(green_ref[u], fy_ref[...], preferred_element_type=jnp.float32)
            send[u] = half.astype(jnp.bfloat16).reshape(parts, piece, width)
            spread_out(0, send, there, u)
            return carry

        lax.fori_loop(0, steps, forward, 0)

        def screen(u, carry):
            wait_for(there.at[u], parts - 1, recv_sem.at[0, u])

            def block(j, inner):
                at = pl.ds(pl.multiple_of(j * (group * xl), group * xl), group * xl)
                there[u, :, at] = screened_block(
                    there[u, :, at], screen_ref, fx_ref, ix_ref, u, j * group, group, parts
                )
                return inner

            lax.fori_loop(0, pairs // group, block, 0)
            spread_out(1, there, here, u)
            return carry

        lax.fori_loop(0, steps, screen, 0)
        total[...] = jnp.zeros(total.shape, jnp.float32)

        def remember(u, carry):
            values = jnp.dot(green_ref[u], spread_ref[...], preferred_element_type=jnp.float32)
            gre[0] = values[:, :width].reshape(NO, NO, xl, width)
            gre[1] = values[:, width:].reshape(NO, NO, xl, width)
            wait_for(here.at[u], parts - 1, recv_sem.at[1, u])
            values = jnp.dot(
                here[u].reshape(rows, width), iy_ref[...], preferred_element_type=jnp.float32
            )
            sig[0] = values[:, :width].reshape(NO, NO, xl, width)
            sig[1] = values[:, width:].reshape(NO, NO, xl, width)

            def tile(n, inner):
                a0 = n // (NO // tb) * ta
                b0 = n % (NO // tb) * tb
                acc = [[total[a0 + i, b0 + j] for j in range(tb)] for i in range(ta)]
                for c in range(NO):
                    s = [sig[0, a0 + i, c] for i in range(ta)]
                    t = [sig[1, a0 + i, c] for i in range(ta)]
                    for j in range(tb):
                        g = gre[0, b0 + j, c]
                        h = gre[1, b0 + j, c]
                        for i in range(ta):
                            acc[i][j] = acc[i][j] + s[i] * g + t[i] * h
                for i in range(ta):
                    for j in range(tb):
                        total[a0 + i, b0 + j] = acc[i][j]
                return inner

            lax.fori_loop(0, NO * NO // (ta * tb), tile, 0)
            return carry

        lax.fori_loop(0, steps, remember, 0)

        for k in range(1, hist):
            other = lax.rem(mine + k, hist)
            pltpu.make_async_remote_copy(
                src_ref=total.at[pl.ds(other * quarter, quarter)],
                dst_ref=sums.at[mine],
                send_sem=hsend_sem.at[0],
                recv_sem=hrecv_sem.at[0],
                device_id={"ha": other},
                device_id_type=mesh_id,
            ).start()
        sums[mine] = total[pl.ds(mine * quarter, quarter)]
        wait_for(sums, hist - 1, hrecv_sem.at[0])
        whole = sums[0]
        for k in range(1, hist):
            whole = whole + sums[k]
        at = pl.ds(pl.multiple_of(mine * qrows, qrows), qrows)
        kernel = base_ref[at] + step_size * whole.reshape(qrows, width)
        final[mine] = kernel.astype(jnp.bfloat16)
        for k in range(1, hist):
            other = lax.rem(mine + k, hist)
            pltpu.make_async_remote_copy(
                src_ref=final.at[mine],
                dst_ref=final.at[mine],
                send_sem=hsend_sem.at[1],
                recv_sem=hrecv_sem.at[1],
                device_id={"ha": other},
                device_id_type=mesh_id,
            ).start()
        wait_for(final, hist - 1, hrecv_sem.at[1])
        out_ref[...] = final[...].reshape(rows, width)
        wait_for(sums, hist - 1, hsend_sem.at[0])
        wait_for(final, hist - 1, hsend_sem.at[1])

        def drain(u, carry):
            wait_for(send.at[u], parts - 1, send_sem.at[0, u])
            wait_for(there.at[u], parts - 1, send_sem.at[1, u])
            return carry

        lax.fori_loop(0, steps, drain, 0)

    blocks = pltpu.VMEM((steps, parts, piece, width), jnp.bfloat16)
    field = pltpu.VMEM((2, NO, NO, xl, width), jnp.float32)
    return pl.pallas_call(
        body,
        in_specs=[pl.BlockSpec(memory_space=pltpu.VMEM)] * 8,
        out_specs=pl.BlockSpec(memory_space=pltpu.VMEM),
        out_shape=jax.ShapeDtypeStruct((rows, width), jnp.bfloat16),
        scratch_shapes=[
            blocks,
            blocks,
            blocks,
            field,
            field,
            pltpu.VMEM((NO, NO, xl, width), jnp.float32),
            pltpu.VMEM((hist, quarter, NO, xl, width), jnp.float32),
            pltpu.VMEM((hist, qrows, width), jnp.bfloat16),
            pltpu.SemaphoreType.DMA((2, steps)),
            pltpu.SemaphoreType.DMA((2, steps)),
            pltpu.SemaphoreType.DMA((2,)),
            pltpu.SemaphoreType.DMA((2,)),
        ],
        compiler_params=params(collective_id=0, has_side_effects=True),
        cost_estimate=cost(100 * steps * rows * width * width, 4 * steps * rows * width),
        name="time_kernel",
    )(green, screened, base, forward_y, inverse_y, spread, forward_x, inverse_x)


def advance(kernel, green, spread):
    steps, rows, width = green.shape
    xl = rows // (NO * NO)
    middle = width // 2
    ta, tc = 4, 8

    def body(kernel_ref, green_ref, spread_ref, out_ref, ker, gre, new):
        @pl.when(pl.program_id(0) == 0)
        def _():
            low = lax.broadcasted_iota(jnp.int32, (rows, width), 1) < middle
            kernel = kernel_ref[...].astype(jnp.float32)
            turned = pltpu.roll(kernel, middle, 1)
            ker[0] = jnp.where(low, kernel, turned).reshape(NO, NO, xl, width)
            ker[1] = jnp.where(low, -turned, kernel).reshape(NO, NO, xl, width)

        values = jnp.dot(green_ref[0], spread_ref[...], preferred_element_type=jnp.float32)
        gre[0] = values[:, :width].reshape(NO, NO, xl, width)
        gre[1] = values[:, width:].reshape(NO, NO, xl, width)

        def tile(n, carry):
            a0 = n // (NO // tc) * ta
            c0 = n % (NO // tc) * tc
            acc = [[jnp.zeros((xl, width), jnp.float32) for j in range(tc)] for i in range(ta)]
            for b in range(NO):
                s = [ker[0, a0 + i, b] for i in range(ta)]
                t = [ker[1, a0 + i, b] for i in range(ta)]
                for j in range(tc):
                    g = gre[0, b, c0 + j]
                    h = gre[1, b, c0 + j]
                    for i in range(ta):
                        acc[i][j] = acc[i][j] + s[i] * g + t[i] * h
            for i in range(ta):
                for j in range(tc):
                    new[a0 + i, c0 + j] = acc[i][j]
            return carry

        lax.fori_loop(0, NO * NO // (ta * tc), tile, 0)
        out_ref[0] = new[...].reshape(rows, width).astype(jnp.bfloat16)

    return pl.pallas_call(
        body,
        grid=(steps,),
        in_specs=[
            pl.BlockSpec((rows, width), lambda i: (0, 0)),
            pl.BlockSpec((1, rows, width), lambda i: (i, 0, 0)),
            pl.BlockSpec((width, 2 * width), lambda i: (0, 0)),
        ],
        out_specs=pl.BlockSpec((1, rows, width), lambda i: (i, 0, 0)),
        out_shape=jax.ShapeDtypeStruct(green.shape, jnp.bfloat16),
        scratch_shapes=[
            pltpu.VMEM((2, NO, NO, xl, width), jnp.float32),
            pltpu.VMEM((2, NO, NO, xl, width), jnp.float32),
            pltpu.VMEM((NO, NO, xl, width), jnp.float32),
        ],
        compiler_params=params(),
        cost_estimate=cost(40 * steps * rows * width * width, 4 * steps * rows * width),
        name="advance",
    )(kernel, green, spread)


def by_kernels(parts, hist, green_row, screened, propagator):
    steps, pairs, xl, width = green_row.shape
    middle = width // 2
    rows = pairs * xl
    cos_y, sin_y = tables(NKY)
    cos_x, sin_x = tables(NKX)
    forward_y = row_matrix(cos_y, sin_y, True)
    inverse_y = row_matrix(cos_y, sin_y, False)
    inverse_y = jnp.concatenate([inverse_y, swap_columns(inverse_y)], axis=1)
    forward_x = jnp.concatenate([cos_x, sin_x], axis=1)
    inverse_x = jnp.concatenate([cos_x, -sin_x], axis=1)
    one = jnp.eye(width, dtype=jnp.bfloat16)
    real, imag = one[:, :middle], one[:, middle:]
    conjugate = jnp.concatenate([real, real, imag, -imag], axis=1)
    crossed = jnp.concatenate([real, imag, imag, real], axis=1)

    green = green_row.reshape(steps, rows, width)
    kernel = time_kernel(
        parts,
        hist,
        green,
        screened,
        propagator.reshape(rows, width),
        forward_y,
        inverse_y,
        conjugate,
        forward_x,
        inverse_x,
    )
    new = advance(kernel, green, crossed)
    return new.reshape(steps, pairs, xl, width)


def by_operations(green_row, screened, propagator):
    steps_local, pairs, rows_local, columns = green_row.shape
    half_width = columns // 2
    cos_y, sin_y = tables(NKY)
    cos_x, sin_x = tables(NKX)
    forward_y = row_matrix(cos_y, sin_y, True)
    inverse_y = row_matrix(cos_y, sin_y, False)
    stacked_x = jnp.concatenate([cos_x, sin_x], axis=1)
    count_x = cos_x.shape[0]
    moved = lax.all_to_all(green_row, "ka", split_axis=1, concat_axis=2, tiled=True)
    half = jnp.einsum("spxw,wv->spxv", moved, forward_y, preferred_element_type=jnp.float32).astype(
        jnp.bfloat16
    )
    both = jnp.einsum("spxw,xz->spwz", half, stacked_x, preferred_element_type=jnp.float32)
    first = both[..., :count_x]
    second = both[..., count_x:]
    space_re = first[:, :, :half_width] - second[:, :, half_width:]
    space_im = first[:, :, half_width:] + second[:, :, :half_width]
    screen_turned = jnp.swapaxes(screened, 2, 3).astype(jnp.float32)
    screen_re = screen_turned[:, :, :half_width]
    screen_im = screen_turned[:, :, half_width:]
    product = jnp.concatenate(
        [space_re * screen_re - space_im * screen_im, space_re * screen_im + space_im * screen_re],
        axis=2,
    ).astype(jnp.bfloat16)
    both_back = jnp.einsum("spwz,zx->spwx", product, stacked_x, preferred_element_type=jnp.float32)
    first_back = both_back[..., :count_x]
    second_back = both_back[..., count_x:]
    back = jnp.concatenate(
        [
            first_back[:, :, :half_width] + second_back[:, :, half_width:],
            first_back[:, :, half_width:] - second_back[:, :, :half_width],
        ],
        axis=2,
    ).astype(jnp.bfloat16)
    sigma_pairs = jnp.einsum(
        "spwx,wv->spxv", back, inverse_y, preferred_element_type=jnp.float32
    ).astype(jnp.bfloat16)
    sigma = lax.all_to_all(sigma_pairs, "ka", split_axis=2, concat_axis=1, tiled=True)
    orbital_shape = (steps_local, NO, NO, rows_local, columns)
    sigma = sigma.reshape(orbital_shape)
    green = green_row.reshape(orbital_shape)
    sigma_re = sigma[..., :half_width]
    sigma_im = sigma[..., half_width:]
    green_re = green[..., :half_width]
    green_im = green[..., half_width:]
    form = "uacxw,ubcxw->abxw"

    def contract(left, right):
        return jnp.einsum(form, left, right, preferred_element_type=jnp.float32)

    memory_re = contract(sigma_re, green_re) + contract(sigma_im, green_im)
    memory_im = contract(sigma_im, green_re) - contract(sigma_re, green_im)
    local_memory = -step_size * jnp.concatenate([memory_re, memory_im], axis=-1)
    base = propagator.reshape(NO, NO, rows_local, columns)
    memory = lax.psum(local_memory, "ha")
    kernel = (base - memory).astype(jnp.bfloat16)
    kernel_re = kernel[..., :half_width]
    kernel_im = kernel[..., half_width:]
    apply_form = "abxw,ubcxw->uacxw"

    def apply_kernel(left, right):
        return jnp.einsum(apply_form, left, right, preferred_element_type=jnp.float32)

    new_re = apply_kernel(kernel_re, green_re) - apply_kernel(kernel_im, green_im)
    new_im = apply_kernel(kernel_re, green_im) + apply_kernel(kernel_im, green_re)
    result = jnp.concatenate([new_re, new_im], axis=-1)
    return result.astype(jnp.bfloat16).reshape(steps_local, pairs, rows_local, columns)


def on_device(parts, hist, green_row, screened, propagator):
    steps, pairs, xl, width = green_row.shape
    if xl % 8 or width != 128 or NO % hist or pairs % (2 * parts):
        return by_operations(green_row, screened, propagator)
    return by_kernels(parts, hist, green_row, screened, propagator)


def solution(mesh):
    in_specs = (P("ha", None, "ka", None), P("ha", "ka", None, None), P(None, "ka", None))
    out_specs = P("ha", None, "ka", None)
    return jax.shard_map(
        functools.partial(on_device, mesh.shape["ka"], mesh.shape["ha"]),
        mesh=mesh,
        in_specs=in_specs,
        out_specs=out_specs,
        check_vma=False,
    )
```

```python
import functools
import math

import jax
import jax.numpy as jnp
from jax import lax
from jax.experimental import pallas as pl
from jax.experimental.pallas import tpu as pltpu
from jax.sharding import PartitionSpec as P

NO = 16
NKX = 64
NKY = 64
VMEM_LIMIT = 58 * 1024 * 1024


step_size = 0.004


def tables(count):
    index = jnp.arange(count, dtype=jnp.int32)
    product = index[:, None] * index[None, :] % count
    angle = product.astype(jnp.float32) * (2.0 * math.pi / count)
    scale = 1.0 / math.sqrt(count)
    return (
        (jnp.cos(angle) * scale).astype(jnp.bfloat16),
        (jnp.sin(angle) * scale).astype(jnp.bfloat16),
    )


def row_matrix(cosine, sine, forward):
    signed = sine if forward else -sine
    upper = jnp.concatenate([cosine, signed], axis=1)
    lower = jnp.concatenate([-signed, cosine], axis=1)
    return jnp.concatenate([upper, lower], axis=0)


def swap_columns(matrix):
    half = matrix.shape[1] // 2
    return jnp.concatenate([matrix[:, half:], matrix[:, :half]], axis=1)


def params(**more):
    return pltpu.CompilerParams(vmem_limit_bytes=VMEM_LIMIT, **more)


def cost(flops, bytes_accessed):
    return pl.CostEstimate(flops=flops, bytes_accessed=bytes_accessed, transcendentals=0)


def screened_block(field, screen_ref, forward_ref, inverse_ref, u, first, group, parts):
    full_x, width = screen_ref.shape[2:]
    xl = full_x // parts
    middle = width // 2
    low = lax.broadcasted_iota(jnp.int32, (full_x, width), 1) < middle
    field = field.astype(jnp.float32).reshape(parts, group, xl, width)
    backs = []
    for pair in range(0, group, 2):
        columns = []
        for k in (pair, pair + 1):
            x = field[:, k].reshape(full_x, width)
            turned = pltpu.roll(x, middle, 1)
            turned = jnp.where(low, -turned, turned)
            columns.append(jnp.concatenate([x, turned], axis=0).astype(jnp.bfloat16))
        stacked = jnp.concatenate(columns, axis=1)
        space = jnp.dot(forward_ref[...], stacked, preferred_element_type=jnp.float32)
        columns = []
        for j in range(2):
            s = space[:, j * width : (j + 1) * width]
            w = screen_ref[u, first + pair + j].astype(jnp.float32)
            direct = s * w
            crossed = s * pltpu.roll(w, middle, 1)
            moved = pltpu.roll(jnp.where(low, crossed, -direct), middle, 1)
            prod = jnp.where(low, direct, crossed) + moved
            turned = pltpu.roll(prod, middle, 1)
            turned = jnp.where(low, -turned, turned)
            columns.append(jnp.concatenate([prod, turned], axis=0).astype(jnp.bfloat16))
        stacked = jnp.concatenate(columns, axis=1)
        back = jnp.dot(inverse_ref[...], stacked, preferred_element_type=jnp.float32)
        for j in range(2):
            backs.append(back[:, j * width : (j + 1) * width].reshape(parts, 1, xl, width))
    out = jnp.concatenate(backs, axis=1).reshape(parts, group * xl, width)
    return out.astype(jnp.bfloat16)


def time_kernel(parts, hist, green, screened, base, forward_y, inverse_y, spread, forward_x, inverse_x):
    steps, rows, width = green.shape
    pairs = screened.shape[1]
    piece = rows // parts
    xl = rows // (NO * NO)
    group = min(16, pairs)
    ta, tb = 4, 8
    quarter = NO // hist
    qrows = rows // hist
    mesh_id = pl.DeviceIdType.MESH

    def body(
        green_ref, screen_hbm, base_ref, fy_ref, iy_ref, spread_ref, fx_ref, ix_ref, out_ref,
        send, there, here, sig, gre, total, sums, final, send_sem, recv_sem, hsend_sem, hrecv_sem,
        screen_ref, load_sem,
    ):
        load = pltpu.make_async_copy(screen_hbm, screen_ref, load_sem)
        load.start()
        me = lax.axis_index("ka")
        mine = lax.axis_index("ha")
        barrier = pltpu.get_barrier_semaphore()
        for k in range(1, parts):
            pl.semaphore_signal(
                barrier, inc=1, device_id={"ka": lax.rem(me + k, parts)}, device_id_type=mesh_id
            )
        for k in range(1, hist):
            pl.semaphore_signal(
                barrier, inc=1, device_id={"ha": lax.rem(mine + k, hist)}, device_id_type=mesh_id
            )
        pl.semaphore_wait(barrier, parts + hist - 2)

        def spread_out(phase, source, target, u):
            target[u, me] = source[u, me]
            for k in range(1, parts):
                other = lax.rem(me + k, parts)
                pltpu.make_async_remote_copy(
                    src_ref=source.at[u, other],
                    dst_ref=target.at[u, me],
                    send_sem=send_sem.at[phase, u],
                    recv_sem=recv_sem.at[phase, u],
                    device_id={"ka": other},
                    device_id_type=mesh_id,
                ).start()

        def wait_for(ref, count, sem):
            pltpu.make_async_copy(ref.at[pl.ds(0, count)], ref.at[pl.ds(0, count)], sem).wait()

        def forward(u, carry):
            half = jnp.dot(green_ref[u], fy_ref[...], preferred_element_type=jnp.float32)
            send[u] = half.astype(jnp.bfloat16).reshape(parts, piece, width)
            spread_out(0, send, there, u)
            return carry

        lax.fori_loop(0, steps, forward, 0)

        def screen(u, carry):
            wait_for(there.at[u], parts - 1, recv_sem.at[0, u])

            def block(j, inner):
                at = pl.ds(pl.multiple_of(j * (group * xl), group * xl), group * xl)
                there[u, :, at] = screened_block(
                    there[u, :, at], screen_ref, fx_ref, ix_ref, u, j * group, group, parts
                )
                return inner

            lax.fori_loop(0, pairs // group, block, 0)
            spread_out(1, there, here, u)
            return carry

        load.wait()
        lax.fori_loop(0, steps, screen, 0)
        total[...] = jnp.zeros(total.shape, jnp.float32)

        def remember(u, carry):
            values = jnp.dot(green_ref[u], spread_ref[...], preferred_element_type=jnp.float32)
            gre[0] = values[:, :width].reshape(NO, NO, xl, width)
            gre[1] = values[:, width:].reshape(NO, NO, xl, width)
            wait_for(here.at[u], parts - 1, recv_sem.at[1, u])
            values = jnp.dot(
                here[u].reshape(rows, width), iy_ref[...], preferred_element_type=jnp.float32
            )
            sig[0] = values[:, :width].reshape(NO, NO, xl, width)
            sig[1] = values[:, width:].reshape(NO, NO, xl, width)

            def tile(n, inner):
                a0 = n // (NO // tb) * ta
                b0 = n % (NO // tb) * tb
                acc = [[total[a0 + i, b0 + j] for j in range(tb)] for i in range(ta)]
                for c in range(NO):
                    s = [sig[0, a0 + i, c] for i in range(ta)]
                    t = [sig[1, a0 + i, c] for i in range(ta)]
                    for j in range(tb):
                        g = gre[0, b0 + j, c]
                        h = gre[1, b0 + j, c]
                        for i in range(ta):
                            acc[i][j] = acc[i][j] + s[i] * g + t[i] * h
                for i in range(ta):
                    for j in range(tb):
                        total[a0 + i, b0 + j] = acc[i][j]
                return inner

            lax.fori_loop(0, NO * NO // (ta * tb), tile, 0)
            return carry

        lax.fori_loop(0, steps, remember, 0)

        for k in range(1, hist):
            other = lax.rem(mine + k, hist)
            pltpu.make_async_remote_copy(
                src_ref=total.at[pl.ds(other * quarter, quarter)],
                dst_ref=sums.at[mine],
                send_sem=hsend_sem.at[0],
                recv_sem=hrecv_sem.at[0],
                device_id={"ha": other},
                device_id_type=mesh_id,
            ).start()
        sums[mine] = total[pl.ds(mine * quarter, quarter)]
        wait_for(sums, hist - 1, hrecv_sem.at[0])
        whole = sums[0]
        for k in range(1, hist):
            whole = whole + sums[k]
        at = pl.ds(pl.multiple_of(mine * qrows, qrows), qrows)
        kernel = base_ref[at] + step_size * whole.reshape(qrows, width)
        final[mine] = kernel.astype(jnp.bfloat16)
        for k in range(1, hist):
            other = lax.rem(mine + k, hist)
            pltpu.make_async_remote_copy(
                src_ref=final.at[mine],
                dst_ref=final.at[mine],
                send_sem=hsend_sem.at[1],
                recv_sem=hrecv_sem.at[1],
                device_id={"ha": other},
                device_id_type=mesh_id,
            ).start()
        wait_for(final, hist - 1, hrecv_sem.at[1])
        out_ref[...] = final[...].reshape(rows, width)
        wait_for(sums, hist - 1, hsend_sem.at[0])
        wait_for(final, hist - 1, hsend_sem.at[1])

        def drain(u, carry):
            wait_for(send.at[u], parts - 1, send_sem.at[0, u])
            wait_for(there.at[u], parts - 1, send_sem.at[1, u])
            return carry

        lax.fori_loop(0, steps, drain, 0)

    blocks = pltpu.VMEM((steps, parts, piece, width), jnp.bfloat16)
    field = pltpu.VMEM((2, NO, NO, xl, width), jnp.float32)
    return pl.pallas_call(
        body,
        in_specs=[pl.BlockSpec(memory_space=pl.ANY if k == 1 else pltpu.VMEM) for k in range(8)],
        out_specs=pl.BlockSpec(memory_space=pltpu.VMEM),
        out_shape=jax.ShapeDtypeStruct((rows, width), jnp.bfloat16),
        scratch_shapes=[
            blocks,
            blocks,
            blocks,
            field,
            field,
            pltpu.VMEM((NO, NO, xl, width), jnp.float32),
            pltpu.VMEM((hist, quarter, NO, xl, width), jnp.float32),
            pltpu.VMEM((hist, qrows, width), jnp.bfloat16),
            pltpu.SemaphoreType.DMA((2, steps)),
            pltpu.SemaphoreType.DMA((2, steps)),
            pltpu.SemaphoreType.DMA((2,)),
            pltpu.SemaphoreType.DMA((2,)),
            pltpu.VMEM(screened.shape, screened.dtype),
            pltpu.SemaphoreType.DMA,
        ],
        compiler_params=params(collective_id=0, has_side_effects=True),
        cost_estimate=cost(100 * steps * rows * width * width, 4 * steps * rows * width),
        name="time_kernel",
    )(green, screened, base, forward_y, inverse_y, spread, forward_x, inverse_x)


def advance(kernel, green, spread):
    steps, rows, width = green.shape
    xl = rows // (NO * NO)
    middle = width // 2
    ta, tc = 4, 8

    tiles = NO * NO // (ta * tc)
    share = NO // tiles

    def body(kernel_ref, green_ref, next_ref, spread_ref, out_ref, ker, gre):
        now = pl.program_id(0) % 2

        @pl.when(pl.program_id(0) == 0)
        def _():
            low = lax.broadcasted_iota(jnp.int32, (rows, width), 1) < middle
            kernel = kernel_ref[...].astype(jnp.float32)
            turned = pltpu.roll(kernel, middle, 1)
            ker[0] = jnp.where(low, kernel, turned).reshape(NO, NO, xl, width)
            ker[1] = jnp.where(low, -turned, kernel).reshape(NO, NO, xl, width)

            values = jnp.dot(green_ref[0], spread_ref[...], preferred_element_type=jnp.float32)
            gre[0, 0] = values[:, :width].reshape(NO, NO, xl, width)
            gre[0, 1] = values[:, width:].reshape(NO, NO, xl, width)

        def tile(n, carry):
            a0 = n // (NO // tc) * ta
            c0 = n % (NO // tc) * tc
            part = pl.ds(pl.multiple_of(n * (rows // tiles), rows // tiles), rows // tiles)
            values = jnp.dot(next_ref[0, part], spread_ref[...], preferred_element_type=jnp.float32)
            shape = (share, NO, xl, width)
            gre[1 - now, 0, pl.ds(n * share, share)] = values[:, :width].reshape(shape)
            gre[1 - now, 1, pl.ds(n * share, share)] = values[:, width:].reshape(shape)
            acc = [[jnp.zeros((xl, width), jnp.float32) for j in range(tc)] for i in range(ta)]
            for b in range(NO):
                s = [ker[0, a0 + i, b] for i in range(ta)]
                t = [ker[1, a0 + i, b] for i in range(ta)]
                for j in range(tc):
                    g = gre[now, 0, b, c0 + j]
                    h = gre[now, 1, b, c0 + j]
                    for i in range(ta):
                        acc[i][j] = acc[i][j] + s[i] * g + t[i] * h
            for i in range(ta):
                at = pl.multiple_of(((a0 + i) * NO + c0) * xl, tc * xl)
                tile_rows = jnp.concatenate(acc[i], axis=0).astype(jnp.bfloat16)
                out_ref[0, pl.ds(at, tc * xl)] = tile_rows
            return carry

        lax.fori_loop(0, tiles, tile, 0)

    return pl.pallas_call(
        body,
        grid=(steps,),
        in_specs=[
            pl.BlockSpec((rows, width), lambda i: (0, 0)),
            pl.BlockSpec((1, rows, width), lambda i: (i, 0, 0)),
            pl.BlockSpec((1, rows, width), lambda i: (jnp.minimum(i + 1, steps - 1), 0, 0)),
            pl.BlockSpec((width, 2 * width), lambda i: (0, 0)),
        ],
        out_specs=pl.BlockSpec((1, rows, width), lambda i: (i, 0, 0)),
        out_shape=jax.ShapeDtypeStruct(green.shape, jnp.bfloat16),
        scratch_shapes=[
            pltpu.VMEM((2, NO, NO, xl, width), jnp.float32),
            pltpu.VMEM((2, 2, NO, NO, xl, width), jnp.float32),
        ],
        compiler_params=params(),
        cost_estimate=cost(40 * steps * rows * width * width, 4 * steps * rows * width),
        name="advance",
    )(kernel, green, green, spread)


def by_kernels(parts, hist, green_row, screened, propagator):
    steps, pairs, xl, width = green_row.shape
    middle = width // 2
    rows = pairs * xl
    cos_y, sin_y = tables(NKY)
    cos_x, sin_x = tables(NKX)
    forward_y = row_matrix(cos_y, sin_y, True)
    inverse_y = row_matrix(cos_y, sin_y, False)
    inverse_y = jnp.concatenate([inverse_y, swap_columns(inverse_y)], axis=1)
    forward_x = jnp.concatenate([cos_x, sin_x], axis=1)
    inverse_x = jnp.concatenate([cos_x, -sin_x], axis=1)
    one = jnp.eye(width, dtype=jnp.bfloat16)
    real, imag = one[:, :middle], one[:, middle:]
    conjugate = jnp.concatenate([real, real, imag, -imag], axis=1)
    crossed = jnp.concatenate([real, imag, imag, real], axis=1)

    green = green_row.reshape(steps, rows, width)
    kernel = time_kernel(
        parts,
        hist,
        green,
        screened,
        propagator.reshape(rows, width),
        forward_y,
        inverse_y,
        conjugate,
        forward_x,
        inverse_x,
    )
    new = advance(kernel, green, crossed)
    return new.reshape(steps, pairs, xl, width)


def by_operations(green_row, screened, propagator):
    steps_local, pairs, rows_local, columns = green_row.shape
    half_width = columns // 2
    cos_y, sin_y = tables(NKY)
    cos_x, sin_x = tables(NKX)
    forward_y = row_matrix(cos_y, sin_y, True)
    inverse_y = row_matrix(cos_y, sin_y, False)
    stacked_x = jnp.concatenate([cos_x, sin_x], axis=1)
    count_x = cos_x.shape[0]
    moved = lax.all_to_all(green_row, "ka", split_axis=1, concat_axis=2, tiled=True)
    half = jnp.einsum("spxw,wv->spxv", moved, forward_y, preferred_element_type=jnp.float32).astype(
        jnp.bfloat16
    )
    both = jnp.einsum("spxw,xz->spwz", half, stacked_x, preferred_element_type=jnp.float32)
    first = both[..., :count_x]
    second = both[..., count_x:]
    space_re = first[:, :, :half_width] - second[:, :, half_width:]
    space_im = first[:, :, half_width:] + second[:, :, :half_width]
    screen_turned = jnp.swapaxes(screened, 2, 3).astype(jnp.float32)
    screen_re = screen_turned[:, :, :half_width]
    screen_im = screen_turned[:, :, half_width:]
    product = jnp.concatenate(
        [space_re * screen_re - space_im * screen_im, space_re * screen_im + space_im * screen_re],
        axis=2,
    ).astype(jnp.bfloat16)
    both_back = jnp.einsum("spwz,zx->spwx", product, stacked_x, preferred_element_type=jnp.float32)
    first_back = both_back[..., :count_x]
    second_back = both_back[..., count_x:]
    back = jnp.concatenate(
        [
            first_back[:, :, :half_width] + second_back[:, :, half_width:],
            first_back[:, :, half_width:] - second_back[:, :, :half_width],
        ],
        axis=2,
    ).astype(jnp.bfloat16)
    sigma_pairs = jnp.einsum(
        "spwx,wv->spxv", back, inverse_y, preferred_element_type=jnp.float32
    ).astype(jnp.bfloat16)
    sigma = lax.all_to_all(sigma_pairs, "ka", split_axis=2, concat_axis=1, tiled=True)
    orbital_shape = (steps_local, NO, NO, rows_local, columns)
    sigma = sigma.reshape(orbital_shape)
    green = green_row.reshape(orbital_shape)
    sigma_re = sigma[..., :half_width]
    sigma_im = sigma[..., half_width:]
    green_re = green[..., :half_width]
    green_im = green[..., half_width:]
    form = "uacxw,ubcxw->abxw"

    def contract(left, right):
        return jnp.einsum(form, left, right, preferred_element_type=jnp.float32)

    memory_re = contract(sigma_re, green_re) + contract(sigma_im, green_im)
    memory_im = contract(sigma_im, green_re) - contract(sigma_re, green_im)
    local_memory = -step_size * jnp.concatenate([memory_re, memory_im], axis=-1)
    base = propagator.reshape(NO, NO, rows_local, columns)
    memory = lax.psum(local_memory, "ha")
    kernel = (base - memory).astype(jnp.bfloat16)
    kernel_re = kernel[..., :half_width]
    kernel_im = kernel[..., half_width:]
    apply_form = "abxw,ubcxw->uacxw"

    def apply_kernel(left, right):
        return jnp.einsum(apply_form, left, right, preferred_element_type=jnp.float32)

    new_re = apply_kernel(kernel_re, green_re) - apply_kernel(kernel_im, green_im)
    new_im = apply_kernel(kernel_re, green_im) + apply_kernel(kernel_im, green_re)
    result = jnp.concatenate([new_re, new_im], axis=-1)
    return result.astype(jnp.bfloat16).reshape(steps_local, pairs, rows_local, columns)


def on_device(parts, hist, green_row, screened, propagator):
    steps, pairs, xl, width = green_row.shape
    if xl % 8 or width != 128 or NO % hist or pairs % (2 * parts):
        return by_operations(green_row, screened, propagator)
    return by_kernels(parts, hist, green_row, screened, propagator)


def solution(mesh):
    in_specs = (P("ha", None, "ka", None), P("ha", "ka", None, None), P(None, "ka", None))
    out_specs = P("ha", None, "ka", None)
    return jax.shard_map(
        functools.partial(on_device, mesh.shape["ka"], mesh.shape["ha"]),
        mesh=mesh,
        in_specs=in_specs,
        out_specs=out_specs,
        check_vma=False,
    )
```
